32 devices in a mesh: job: 2 (over y), pole: 4 (over z), col: 4 (over x, core).
Axes of the slice: x: 2, y: 2, z: 4, core: 2. Of those that a mesh axis runs over, the one named last changes fastest.
Arguments:
- inverse: bfloat16 [8, 2, 6144, 6144], P(('job', 'pole'), None, 'col'), parts along dimension 0, may hold values from -6 to 6
- panels: bfloat16 [8, 3, 2, 6144, 128], P(('job', 'pole'), None, None, 'col'), parts along dimension 0, may hold values from -0.078125 to 0.078125
- diag_inverse: float32 [8, 3, 2, 128, 128], P(('job', 'pole')), parts along dimension 0, may hold values from -6 to 6
- pole_weights: float32 [8, 2], P(('job', 'pole')), parts along dimension 0, may hold values from -1 to 1
- supports: int32 [32, 8], replicated, may hold values from 0 to 143, as said below
- counts: int32 [32], replicated, may hold values from 1 to 8, as said below
- panel_order: int32 [3], replicated, may hold values from 0 to 2, each once
- row_orbitals: bfloat16 [64, 8, 128, 512], P(('job', 'col'), None, None, 'pole'), parts along dimension 0, may hold values from -0.5 to 0.5
- panel_orbitals: bfloat16 [64, 3, 128, 512], P(('job', 'col'), None, None, 'pole'), parts along dimension 0, may hold values from -0.078125 to 0.078125
- core_density: float32 [64, 512], P(('job', 'col'), 'pole'), parts along dimension 0, may hold values from 0.5 to 4
Outputs:
- valence_density: float32 [64, 512], P(('job', 'col'), 'pole'), parts along dimension 0
- exchange_potential: float32 [64, 512], P(('job', 'col'), 'pole'), parts along dimension 0
- diag_density: float32 [6, 128, 128], P('job'), parts along dimension 0
The draws below stay inside these ranges and needn't reach their ends.
There are 2 independent parts, one for each index of `job`. The reference program is written for one: setup_inputs(seed, part) draws one part's arguments, and reference() takes and returns one part's arrays. A program takes and returns all parts, laid end to end along the dimension named above; an argument that names none is the same for every part. Nothing has to cross between parts.
Inputs may be any that keep to these rules, and one draw needn't show every extreme that they name: `supports`: the ids within one tile's list are distinct. Block g belongs to index g // 36 of col. Over the first counts[t] entries of all tiles of one index of col, at most 3 distinct blocks belong to any one index of col, and exactly 3 for some pair in every draw. `counts`: some tile of every index of col has a full list.
All inputs are finite; a program needn't handle non-finite values.
Results may differ from the reference program's by a relative error of at most 0.0029.
Values may be sent and summed in bfloat16 or wider, within the bound.
A program may use at most 128 MiB of HBM per device.

```python
import math
import jax
import jax.numpy as jnp
from jax import lax

M = 6144
W = 128
PANELS = 3
TILE_DEV = 8
S_MAX = 8
CAP = 3
POLES = 4
TILES = 32
R = 512
NB = 144
B_DEV = 36


def support_tables(key):
    base = jax.random.fold_in(key, 4099)
    first_key, second_key, third_key = jax.random.split(base, 3)
    col_count = TILES // TILE_DEV
    pool_size = col_count * CAP
    ranking = jax.random.randint(first_key, (col_count, col_count, B_DEV), 0, 1 << 20) * B_DEV + jnp.arange(B_DEV, dtype=jnp.int32)
    allowed = jnp.argsort(ranking, axis=-1)[:, :, :CAP].astype(jnp.int32)
    tile_ids = jnp.arange(TILES, dtype=jnp.int32)
    owner_dest = tile_ids // TILE_DEV
    item_ids = jnp.arange(pool_size, dtype=jnp.int32)
    source_of = item_ids // CAP
    forced = (tile_ids % TILE_DEV == 0)[:, None] & (source_of[None, :] == ((owner_dest + 1) % col_count)[:, None])
    scores = jax.random.randint(second_key, (TILES, pool_size), 0, 1 << 20) * pool_size + item_ids[None, :] + pool_size
    scores = jnp.where(forced, item_ids[None, :], scores)
    picked_items = jnp.argsort(scores, axis=1)[:, :S_MAX].astype(jnp.int32)
    sources = picked_items // CAP
    ranks = picked_items % CAP
    local_pick = allowed[owner_dest[:, None], sources, ranks]
    support_ids = (sources * B_DEV + local_pick).astype(jnp.int32)
    lengths = jax.random.randint(third_key, (TILES,), 1, S_MAX + 1)
    lengths = jnp.where(tile_ids % TILE_DEV == 0, S_MAX, lengths).astype(jnp.int32)
    return (support_ids, lengths)


def draw_supports(key, part):
    return support_tables(key)[0]


def draw_counts(key, part):
    return support_tables(key)[1]


def block_scale(rng, shape, cuts, low, high):
    def one(axis_at, shards_of):
        draws = jax.random.uniform(jax.random.fold_in(jax.random.fold_in(rng, 6), axis_at), (shards_of,), jnp.float32, low / len(cuts), high / len(cuts))
        return jnp.repeat(jnp.exp(draws), shape[axis_at] // shards_of).reshape((-1,) + (1,) * (len(shape) - axis_at - 1))

    level = one(*cuts[0])
    for cut in cuts[1:]:
        level = level * one(*cut)
    return level


def normal_values(rng, shape, scale, reach, cuts=(), kind=jnp.bfloat16):
    drawn = jax.random.normal(rng, shape, jnp.float32) * scale
    if len(cuts) > 0:
        drawn = block_scale(rng, shape, cuts, -0.22, 0.18) * drawn
    return jnp.clip(drawn, min=-reach, max=reach).astype(kind)


def setup_inputs(seed: int = 0, part: int = 0) -> dict:
    keys = jax.random.split(jax.random.key(seed), 11)
    part_splits = jax.random.split(jax.random.fold_in(keys[10], part), 11)
    inverse = normal_values(part_splits[0], (POLES, 2, M, M), 1.0, 6.0, ((0, 4), (2, 4)))
    panels = normal_values(part_splits[1], (POLES, PANELS, 2, M, W), M ** -0.5, 0.078125, ((0, 4), (3, 4)))
    diag_inverse = normal_values(part_splits[2], (POLES, PANELS, 2, W, W), 1.0, 6.0, ((0, 4),), jnp.float32)
    pole_weights = jnp.clip(jax.random.uniform(part_splits[3], (POLES, 2), jnp.float32, -1.0, 1.0) * block_scale(part_splits[3], (POLES, 2), ((0, 4),), -0.4, 0.0), -1.0, 1.0)
    supports = draw_supports(jax.random.fold_in(keys[10], 71), part)
    counts = draw_counts(jax.random.fold_in(keys[10], 71), part)
    panel_order = jax.random.permutation(keys[6], PANELS).astype(jnp.int32)
    row_orbitals = normal_values(part_splits[7], (TILES, S_MAX, W, R), W ** -0.5, 0.5, ((0, 4), (3, 4)))
    panel_orbitals = normal_values(part_splits[8], (TILES, PANELS, W, R), (W * 48) ** -0.5, 0.078125, ((0, 4), (3, 4)))
    core_density = jnp.clip(jnp.exp(math.log(4.0) - 2.0794415 * jax.random.uniform(part_splits[9], (TILES, R), jnp.float32) ** block_scale(part_splits[9], (TILES, R), ((0, 4), (1, 4)), -0.2, 0.2)), 0.5, 4.0)
    return {"inverse": inverse, "panels": panels, "diag_inverse": diag_inverse, "pole_weights": pole_weights, "supports": supports, "counts": counts, "panel_order": panel_order, "row_orbitals": row_orbitals, "panel_orbitals": panel_orbitals, "core_density": core_density}


exchange_coeff = (3.0 / 3.141592653589793) ** (1.0 / 3.0)
density_floor = 0.5


def reference(inverse, panels, diag_inverse, pole_weights, supports, counts, panel_order, row_orbitals, panel_orbitals, core_density):
    order_list = panel_order

    def scan_step(carry, items):
        inverse_pole, panels_pole, diag_pole, weight = items
        ordered = jnp.take(panels_pole, order_list, axis=0)
        diag_ordered = jnp.take(diag_pole, order_list, axis=0)
        stacked = inverse_pole.reshape(2 * M, M)
        right_side = ordered.transpose(2, 0, 1, 3).reshape(M, PANELS * 2 * W)
        product = jnp.dot(stacked, right_side, preferred_element_type=jnp.float32).reshape(2, M, PANELS, 2, W)
        real_part = -(product[0, :, :, 0] - product[1, :, :, 1])
        imag_part = -(product[0, :, :, 1] + product[1, :, :, 0])
        density = weight[0] * imag_part + weight[1] * real_part
        lower_rows = ordered.astype(jnp.float32)
        highest = lax.Precision.HIGHEST
        cross_real = jnp.einsum("jiw,ijv->jwv", lower_rows[:, 0], real_part, precision=highest) - jnp.einsum("jiw,ijv->jwv", lower_rows[:, 1], imag_part, precision=highest)
        cross_imag = jnp.einsum("jiw,ijv->jwv", lower_rows[:, 0], imag_part, precision=highest) + jnp.einsum("jiw,ijv->jwv", lower_rows[:, 1], real_part, precision=highest)
        diag_term = weight[0] * (diag_ordered[:, 1] - cross_imag) + weight[1] * (diag_ordered[:, 0] - cross_real)
        return (carry[0] + density, carry[1] + diag_term), None

    start = (jnp.zeros((M, PANELS, W), jnp.float32), jnp.zeros((PANELS, W, W), jnp.float32))
    (density, diag_density), unused = lax.scan(scan_step, start, (inverse, panels, diag_inverse, pole_weights))
    density_blocks = density.astype(jnp.bfloat16)
    blocks = density_blocks.reshape(M // W, W, PANELS, W).transpose(0, 2, 1, 3).reshape(NB, W, W)

    def tile_step(items):
        support, count, orbitals, panel_values, core = items
        picked = blocks[support].astype(jnp.float32)
        chosen = panel_values[support % PANELS].astype(jnp.float32)
        mixed = jnp.einsum("kim,kmr->kir", picked, chosen)
        contribution = jnp.sum(orbitals.astype(jnp.float32) * mixed, axis=1)
        live_slots = (jnp.arange(S_MAX, dtype=jnp.int32) < count).astype(jnp.float32)
        valence = jnp.sum(contribution * live_slots[:, None], axis=0)
        clamped = jnp.maximum(core + valence, density_floor)
        return valence, -exchange_coeff * clamped ** (1.0 / 3.0)

    valence_density, exchange_potential = lax.map(tile_step, (supports, counts, row_orbitals, panel_orbitals, core_density))
    return valence_density, exchange_potential, diag_density
```

```python
import functools

import jax
import jax.numpy as jnp
from jax import lax
from jax.experimental import pallas as pl
from jax.experimental.pallas import tpu as pltpu
from jax.sharding import PartitionSpec as P

CAP = 3
CORES = 2
exchange_coeff = (3.0 / 3.141592653589793) ** (1.0 / 3.0)
density_floor = 0.5
MESH = pl.DeviceIdType.MESH


def pick_tile(size, options):
    for option in options:
        if size % option == 0:
            return option
    return size


def panel_kernel(
    cols,
    pieces,
    order_ref,
    chosen_ref,
    weight_ref,
    inverse_ref,
    panels_ref,
    diag_ref,
    blocks_ref,
    diag_out_ref,
    held,
    tiles,
    acc,
    dens,
    cross,
    own_sem,
    tile_sem,
    send_far,
    recv_far,
    send_mate,
    recv_mate,
):
    me = lax.axis_index("col")
    chips = cols // CORES
    my_chip, my_core = me // CORES, me % CORES
    mate = my_chip * CORES + (1 - my_core)
    panel_count, _, rows, width = panels_ref.shape
    piece = rows // pieces
    slots = tiles.shape[0]

    own_copy = pltpu.make_async_copy(panels_ref, held.at[me], own_sem)
    own_copy.start()

    def far_chip(hop):
        return (my_chip + hop) % chips

    steps = [(me, k) for k in range(pieces)]
    steps += [(mate, k) for k in range(pieces)]
    for k in range(pieces):
        for hop in range(1, chips):
            steps.append((far_chip(hop) * CORES + my_core, k))
        for hop in range(1, chips):
            steps.append((far_chip(hop) * CORES + 1 - my_core, k))

    def tile_copy(s):
        owner, k = steps[s]
        start = pl.multiple_of(owner * rows + k * piece, 128)
        return pltpu.make_async_copy(
            inverse_ref.at[:, :, pl.ds(start, piece)], tiles.at[s % slots], tile_sem.at[s % slots]
        )

    for s in range(min(slots - 1, len(steps))):
        tile_copy(s).start()

    barrier = pltpu.get_barrier_semaphore()
    pl.semaphore_signal(barrier, inc=1, device_id={"col": mate}, device_id_type=MESH)
    for hop in range(1, chips):
        pl.semaphore_signal(
            barrier, inc=1, device_id={"col": far_chip(hop) * CORES + my_core}, device_id_type=MESH
        )
    pl.semaphore_wait(barrier, chips)

    def part(ref, k):
        return ref.at[:, :, pl.ds(k * piece, piece), :]

    def far_copy(hop, k):
        return pltpu.make_async_remote_copy(
            src_ref=part(panels_ref, k),
            dst_ref=part(held.at[me], k),
            send_sem=send_far.at[hop, k],
            recv_sem=recv_far.at[hop, k],
            device_id={"col": far_chip(hop) * CORES + my_core},
            device_id_type=MESH,
        )

    def far_arrival(hop, k):
        source = (my_chip + chips - hop) % chips * CORES + my_core
        return source, pltpu.make_async_remote_copy(
            src_ref=part(panels_ref, k),
            dst_ref=part(held.at[source], k),
            send_sem=send_far.at[hop, k],
            recv_sem=recv_far.at[hop, k],
            device_id={"col": source},
            device_id_type=MESH,
        )

    def mate_copy(hop, k):
        source = (my_chip + chips - hop) % chips * CORES + my_core
        src = part(panels_ref, k) if hop == 0 else part(held.at[source], k)
        return pltpu.make_async_remote_copy(
            src_ref=src,
            dst_ref=part(held.at[source], k),
            send_sem=send_mate.at[hop, k],
            recv_sem=recv_mate.at[hop, k],
            device_id={"col": mate},
            device_id_type=MESH,
        )

    def mate_arrival(hop, k):
        source = (my_chip + chips - hop) % chips * CORES + 1 - my_core
        return pltpu.make_async_remote_copy(
            src_ref=part(panels_ref, k),
            dst_ref=part(held.at[source], k),
            send_sem=send_mate.at[hop, k],
            recv_sem=recv_mate.at[hop, k],
            device_id={"col": mate},
            device_id_type=MESH,
        )

    for k in range(pieces):
        for hop in range(1, chips):
            far_copy(hop, k).start()
    for k in range(pieces):
        mate_copy(0, k).start()
    own_copy.wait()

    tall = 2 * rows
    tile_rows = pick_tile(rows, (512, 384, 256, 128))

    far_index = [(hop, k) for k in range(pieces) for hop in range(1, chips)]
    forwarded = []

    for s in range(len(steps)):
        owner, k = steps[s]
        if s + slots - 1 < len(steps):
            tile_copy(s + slots - 1).start()
        group = 2 * (chips - 1)
        if s < pieces:
            pass
        elif s < 2 * pieces:
            mate_arrival(0, k).wait_recv()
        else:
            within = (s - 2 * pieces) % group
            if within == 0:
                for hop in range(1, chips):
                    far_arrival(chips - hop, k)[1].wait_recv()
                    mate_copy(chips - hop, k).start()
                    forwarded.append((chips - hop, k))
            if within >= chips - 1:
                mate_arrival(chips - (within - (chips - 1) + 1), k).wait_recv()
        tile_copy(s).wait()
        slot = s % slots

        def multiply(index, carry, owner=owner, k=k, slot=slot, first=(s == 0)):
            half, at = index // (rows // tile_rows), index % (rows // tile_rows)
            left = tiles[slot, half, pl.ds(at * tile_rows, tile_rows), :]
            out_rows = pl.ds(index * tile_rows, tile_rows)
            for p in range(panel_count):
                right = jnp.concatenate(
                    [held[owner, p, 0, k * piece : (k + 1) * piece, :], held[owner, p, 1, k * piece : (k + 1) * piece, :]],
                    axis=1,
                )
                term = jnp.dot(left, right, preferred_element_type=jnp.float32)
                if first:
                    acc[p, out_rows, :] = term
                else:
                    acc[p, out_rows, :] += term
            return carry

        lax.fori_loop(0, tall // tile_rows, multiply, 0)

    weight_real, weight_imag = weight_ref[0, 0], weight_ref[0, 1]
    cross[...] = jnp.zeros_like(cross)
    block_rows = rows // width

    def finish(b, carry):
        at = pl.ds(b * width, width)
        low = pl.ds(rows + b * width, width)
        for p in range(panel_count):
            top = acc[p, at, :]
            bottom = acc[p, low, :]
            real = bottom[:, width:] - top[:, :width]
            imag = -(top[:, width:] + bottom[:, :width])
            value = weight_real * imag + weight_imag * real
            other = weight_real * real - weight_imag * imag
            dens[p * block_rows + b] = value
            both = jnp.concatenate([value, other], axis=0)
            high = both.astype(jnp.bfloat16)
            rest = (both - high.astype(jnp.float32)).astype(jnp.bfloat16)
            left = jnp.concatenate([held[me, p, 0, at, :], held[me, p, 1, at, :]], axis=0)
            both = lax.dot_general(
                left,
                jnp.concatenate([high, rest], axis=1),
                (((0,), (0,)), ((), ())),
                preferred_element_type=jnp.float32,
            )
            cross[p] += both[:, :width] + both[:, width:]
        return carry

    lax.fori_loop(0, block_rows, finish, 0)
    leading = jnp.where(me == 0, 1.0, 0.0).astype(jnp.float32)
    for j in range(panel_count):
        source = order_ref[j]
        diag_out_ref[j] = (
            leading * (weight_real * diag_ref[source, 1] + weight_imag * diag_ref[source, 0]) - cross[source]
        )
    for c in range(blocks_ref.shape[0]):
        blocks_ref[c] = dens[chosen_ref[c]].astype(blocks_ref.dtype)

    for k in range(pieces):
        for hop in range(1, chips):
            far_copy(hop, k).wait_send()
        mate_copy(0, k).wait_send()
    for hop, k in forwarded:
        mate_copy(hop, k).wait_send()


def tile_kernel(ids_ref, supports_ref, counts_ref, blocks_ref, rows_ref, panels_ref, core_ref, valence_ref, potential_ref):
    tile_count, list_size = rows_ref.shape[0], rows_ref.shape[1]
    panel_count = panels_ref.shape[1]
    id_count = ids_ref.shape[0]

    def one(t, carry):
        total = jnp.zeros((1, rows_ref.shape[3]), jnp.float32)
        count = counts_ref[t]
        for k in range(list_size):
            block = supports_ref[t, k]
            place = jnp.int32(0)
            for c in range(id_count):
                place = jnp.where(ids_ref[c] == block, c, place)
            mixed = jnp.dot(
                blocks_ref[place], panels_ref[t, block % panel_count], preferred_element_type=jnp.float32
            )
            term = jnp.sum(rows_ref[t, k].astype(jnp.float32) * mixed, axis=0, keepdims=True)
            total += jnp.where(k < count, term, 0.0)
        valence_ref[pl.ds(t, 1), :] = total
        return carry

    lax.fori_loop(0, tile_count, one, 0)
    clamped = jnp.maximum(core_ref[...] + valence_ref[...], density_floor)
    potential_ref[...] = -exchange_coeff * jnp.exp(jnp.log(clamped) * (1.0 / 3.0))


def body(
    inverse,
    panels,
    diag_inverse,
    pole_weights,
    supports,
    counts,
    panel_order,
    row_orbitals,
    panel_orbitals,
    core_density,
):
    rows = inverse.shape[2]
    panel_count, width = panels.shape[1], panels.shape[4]
    cols = lax.axis_size("col")
    me = lax.axis_index("col")
    block_rows = rows // width
    per_device = block_rows * panel_count
    tile_count, list_size = row_orbitals.shape[0], row_orbitals.shape[1]
    total = cols * per_device

    all_ids = jnp.arange(total, dtype=jnp.int32)
    live = jnp.arange(list_size, dtype=jnp.int32)[None, :] < counts[:, None]
    listed = jnp.where(live, supports, -1).reshape(cols, tile_count * list_size)
    needed = jnp.any(listed[:, :, None] == all_ids[None, None, :], axis=1)
    before = (all_ids[:, None] < all_ids[None, :]) & (
        all_ids[:, None] // per_device == all_ids[None, :] // per_device
    )
    rank = jnp.sum(jnp.where(needed[:, :, None] & before[None], 1, 0), axis=1)
    slot = jnp.where(needed, all_ids[None, :] // per_device * CAP + rank, -1)
    ids = jnp.max(
        jnp.where(
            slot[:, None, :] == jnp.arange(cols * CAP, dtype=jnp.int32)[None, :, None], all_ids[None, None, :], -1
        ),
        axis=2,
    )
    mine = lax.dynamic_slice_in_dim(ids, me * CAP, CAP, 1).reshape(-1)
    local = jnp.maximum(mine - me * per_device, 0)
    column = local % panel_count
    source = jnp.zeros_like(column)
    for j in range(panel_count):
        source = jnp.where(column == j, panel_order[j], source)
    chosen = source * block_rows + local // panel_count
    my_ids = lax.dynamic_slice_in_dim(ids, me, 1, 0)[0]
    my_supports = lax.dynamic_slice_in_dim(supports, me * tile_count, tile_count, 0)
    my_counts = lax.dynamic_slice_in_dim(counts, me * tile_count, tile_count, 0)

    pieces = rows // 256 if rows % 256 == 0 else 1
    piece = rows // pieces
    chips = cols // CORES
    slots = 4
    smem = pl.BlockSpec(memory_space=pltpu.SMEM)
    vmem = pl.BlockSpec(memory_space=pltpu.VMEM)
    anywhere = pl.BlockSpec(memory_space=pl.ANY)
    blocks, diag_term = pl.pallas_call(
        functools.partial(panel_kernel, cols, pieces),
        out_shape=(
            jax.ShapeDtypeStruct((cols * CAP, width, width), jnp.float32),
            jax.ShapeDtypeStruct((panel_count, width, width), jnp.float32),
        ),
        in_specs=[smem, smem, smem, anywhere, anywhere, vmem],
        out_specs=(vmem, vmem),
        scratch_shapes=[
            pltpu.VMEM((cols, panel_count, 2, rows, width), jnp.bfloat16),
            pltpu.VMEM((slots, 2, rows, piece), jnp.bfloat16),
            pltpu.VMEM((panel_count, 2 * rows, 2 * width), jnp.float32),
            pltpu.VMEM((per_device, width, width), jnp.float32),
            pltpu.VMEM((panel_count, width, width), jnp.float32),
            pltpu.SemaphoreType.DMA,
            pltpu.SemaphoreType.DMA((slots,)),
            pltpu.SemaphoreType.DMA((chips, pieces)),
            pltpu.SemaphoreType.DMA((chips, pieces)),
            pltpu.SemaphoreType.DMA((chips, pieces)),
            pltpu.SemaphoreType.DMA((chips, pieces)),
        ],
        compiler_params=pltpu.CompilerParams(
            collective_id=0, has_side_effects=True, vmem_limit_bytes=48 * 1024 * 1024
        ),
        name="panel_products",
    )(panel_order, chosen, pole_weights, inverse[0], panels[0], diag_inverse[0])

    diag_density = lax.psum(diag_term, ("pole", "col"))
    summed = lax.psum(blocks, "pole").astype(jnp.bfloat16).reshape(cols, CAP, width, width)
    incoming = lax.all_to_all(summed, "col", split_axis=0, concat_axis=0, tiled=True)
    incoming = incoming.reshape(cols * CAP, width, width)
    valence, potential = pl.pallas_call(
        tile_kernel,
        out_shape=(
            jax.ShapeDtypeStruct(core_density.shape, jnp.float32),
            jax.ShapeDtypeStruct(core_density.shape, jnp.float32),
        ),
        in_specs=[smem, smem, smem, vmem, vmem, vmem, vmem],
        out_specs=(vmem, vmem),
        compiler_params=pltpu.CompilerParams(vmem_limit_bytes=24 * 1024 * 1024),
        name="tile_products",
    )(my_ids, my_supports, my_counts, incoming, row_orbitals, panel_orbitals, core_density)
    return (valence, potential, diag_density)


def solution(mesh):
    placed = (
        P(("job", "pole"), None, "col", None),
        P(("job", "pole"), None, None, "col", None),
        P(("job", "pole"), None, None, None, None),
        P(("job", "pole"), None),
        P(),
        P(),
        P(),
        P(("job", "col"), None, None, "pole"),
        P(("job", "col"), None, None, "pole"),
        P(("job", "col"), "pole"),
    )
    return jax.shard_map(
        body,
        mesh=mesh,
        in_specs=placed,
        out_specs=(P(("job", "col"), "pole"), P(("job", "col"), "pole"), P("job", None, None)),
        check_vma=False,
    )
```

```python
import functools

import jax
import jax.numpy as jnp
from jax import lax
from jax.experimental import pallas as pl
from jax.experimental.pallas import tpu as pltpu
from jax.sharding import PartitionSpec as P

CAP = 3
CORES = 2
exchange_coeff = (3.0 / 3.141592653589793) ** (1.0 / 3.0)
density_floor = 0.5
MESH = pl.DeviceIdType.MESH


def pick_tile(size, options):
    for option in options:
        if size % option == 0:
            return option
    return size


def panel_kernel(
    cols,
    pieces,
    order_ref,
    chosen_ref,
    weight_ref,
    inverse_ref,
    panels_ref,
    diag_ref,
    blocks_ref,
    diag_out_ref,
    held,
    tiles,
    acc,
    dens,
    cross,
    own_sem,
    tile_sem,
    send_far,
    recv_far,
    send_mate,
    recv_mate,
):
    me = lax.axis_index("col")
    chips = cols // CORES
    my_chip, my_core = me // CORES, me % CORES
    mate = my_chip * CORES + (1 - my_core)
    panel_count, _, rows, width = panels_ref.shape
    piece = rows // pieces
    slots = tiles.shape[0]

    own_copy = pltpu.make_async_copy(panels_ref, held.at[me], own_sem)
    own_copy.start()

    def far_chip(hop):
        return (my_chip + hop) % chips

    steps = [(me, k) for k in range(pieces)]
    steps += [(mate, k) for k in range(pieces)]
    for k in range(pieces):
        for hop in range(1, chips):
            steps.append((far_chip(hop) * CORES + my_core, k))
        for hop in range(1, chips):
            steps.append((far_chip(hop) * CORES + 1 - my_core, k))

    def tile_copy(s):
        owner, k = steps[s]
        start = pl.multiple_of(owner * rows + k * piece, 128)
        return pltpu.make_async_copy(
            inverse_ref.at[:, :, pl.ds(start, piece)], tiles.at[s % slots], tile_sem.at[s % slots]
        )

    for s in range(min(slots - 1, len(steps))):
        tile_copy(s).start()

    barrier = pltpu.get_barrier_semaphore()
    pl.semaphore_signal(barrier, inc=1, device_id={"col": mate}, device_id_type=MESH)
    for hop in range(1, chips):
        pl.semaphore_signal(
            barrier, inc=1, device_id={"col": far_chip(hop) * CORES + my_core}, device_id_type=MESH
        )
    pl.semaphore_wait(barrier, chips)

    def part(ref, k):
        return ref.at[:, :, pl.ds(k * piece, piece), :]

    def far_copy(hop, k):
        return pltpu.make_async_remote_copy(
            src_ref=part(panels_ref, k),
            dst_ref=part(held.at[me], k),
            send_sem=send_far.at[hop, k],
            recv_sem=recv_far.at[hop, k],
            device_id={"col": far_chip(hop) * CORES + my_core},
            device_id_type=MESH,
        )

    def far_arrival(hop, k):
        source = (my_chip + chips - hop) % chips * CORES + my_core
        return source, pltpu.make_async_remote_copy(
            src_ref=part(panels_ref, k),
            dst_ref=part(held.at[source], k),
            send_sem=send_far.at[hop, k],
            recv_sem=recv_far.at[hop, k],
            device_id={"col": source},
            device_id_type=MESH,
        )

    def mate_copy(hop, k):
        source = (my_chip + chips - hop) % chips * CORES + my_core
        src = part(panels_ref, k) if hop == 0 else part(held.at[source], k)
        return pltpu.make_async_remote_copy(
            src_ref=src,
            dst_ref=part(held.at[source], k),
            send_sem=send_mate.at[hop, k],
            recv_sem=recv_mate.at[hop, k],
            device_id={"col": mate},
            device_id_type=MESH,
        )

    def mate_arrival(hop, k):
        source = (my_chip + chips - hop) % chips * CORES + 1 - my_core
        return pltpu.make_async_remote_copy(
            src_ref=part(panels_ref, k),
            dst_ref=part(held.at[source], k),
            send_sem=send_mate.at[hop, k],
            recv_sem=recv_mate.at[hop, k],
            device_id={"col": mate},
            device_id_type=MESH,
        )

    for k in range(pieces):
        for hop in range(1, chips):
            far_copy(hop, k).start()
    for k in range(pieces):
        mate_copy(0, k).start()
    own_copy.wait()

    tall = 2 * rows
    tile_rows = pick_tile(rows, (512, 384, 256, 128))

    far_index = [(hop, k) for k in range(pieces) for hop in range(1, chips)]
    forwarded = []

    for s in range(len(steps)):
        owner, k = steps[s]
        if s + slots - 1 < len(steps):
            tile_copy(s + slots - 1).start()
        group = 2 * (chips - 1)
        if s < pieces:
            pass
        elif s < 2 * pieces:
            mate_arrival(0, k).wait_recv()
        else:
            within = (s - 2 * pieces) % group
            if within == 0:
                for hop in range(1, chips):
                    far_arrival(chips - hop, k)[1].wait_recv()
                    mate_copy(chips - hop, k).start()
                    forwarded.append((chips - hop, k))
            if within >= chips - 1:
                mate_arrival(chips - (within - (chips - 1) + 1), k).wait_recv()
        tile_copy(s).wait()
        slot = s % slots

        def multiply(index, carry, owner=owner, k=k, slot=slot, first=(s == 0)):
            half, at = index // (rows // tile_rows), index % (rows // tile_rows)
            left = tiles[slot, half, pl.ds(at * tile_rows, tile_rows), :]
            out_rows = pl.ds(index * tile_rows, tile_rows)
            for p in range(panel_count):
                right = jnp.concatenate(
                    [held[owner, p, 0, k * piece : (k + 1) * piece, :], held[owner, p, 1, k * piece : (k + 1) * piece, :]],
                    axis=1,
                )
                term = jnp.dot(left, right, preferred_element_type=jnp.float32)
                if first:
                    acc[p, out_rows, :] = term
                else:
                    acc[p, out_rows, :] += term
            return carry

        lax.fori_loop(0, tall // tile_rows, multiply, 0)

    weight_real, weight_imag = weight_ref[0, 0], weight_ref[0, 1]
    cross[...] = jnp.zeros_like(cross)
    block_rows = rows // width

    def finish(b, carry):
        at = pl.ds(b * width, width)
        low = pl.ds(rows + b * width, width)
        for p in range(panel_count):
            top = acc[p, at, :]
            bottom = acc[p, low, :]
            real = bottom[:, width:] - top[:, :width]
            imag = -(top[:, width:] + bottom[:, :width])
            value = weight_real * imag + weight_imag * real
            other = weight_real * real - weight_imag * imag
            dens[p * block_rows + b] = value
            both = jnp.concatenate([value, other], axis=0)
            high = both.astype(jnp.bfloat16)
            rest = (both - high.astype(jnp.float32)).astype(jnp.bfloat16)
            left = jnp.concatenate([held[me, p, 0, at, :], held[me, p, 1, at, :]], axis=0)
            both = lax.dot_general(
                left,
                jnp.concatenate([high, rest], axis=1),
                (((0,), (0,)), ((), ())),
                preferred_element_type=jnp.float32,
            )
            cross[p] += both[:, :width] + both[:, width:]
        return carry

    lax.fori_loop(0, block_rows, finish, 0)
    leading = jnp.where(me == 0, 1.0, 0.0).astype(jnp.float32)
    for j in range(panel_count):
        source = order_ref[j]
        diag_out_ref[j] = (
            leading * (weight_real * diag_ref[source, 1] + weight_imag * diag_ref[source, 0]) - cross[source]
        )
    for c in range(blocks_ref.shape[0]):
        blocks_ref[c] = dens[chosen_ref[c]].astype(blocks_ref.dtype)

    for k in range(pieces):
        for hop in range(1, chips):
            far_copy(hop, k).wait_send()
        mate_copy(0, k).wait_send()
    for hop, k in forwarded:
        mate_copy(hop, k).wait_send()


def exchange_kernel(
    poles,
    cols,
    ids_ref,
    supports_ref,
    counts_ref,
    blocks_ref,
    diag_ref,
    rows_ref,
    panels_ref,
    core_ref,
    valence_ref,
    potential_ref,
    diag_out_ref,
    block_in,
    block_sum,
    block_full,
    diag_in,
    diag_col,
    diag_full,
    send_a,
    recv_a,
    send_b,
    recv_b,
    send_c,
    recv_c,
    send_d,
    recv_d,
    send_e,
    recv_e,
    send_f,
    recv_f,
):
    pole, col = lax.axis_index("pole"), lax.axis_index("col")
    part = blocks_ref.shape[1] // poles

    barrier = pltpu.get_barrier_semaphore()
    for hop in range(1, poles):
        pl.semaphore_signal(barrier, inc=1, device_id={"pole": (pole + hop) % poles}, device_id_type=MESH)
    for hop in range(1, cols):
        pl.semaphore_signal(barrier, inc=1, device_id={"col": (col + hop) % cols}, device_id_type=MESH)
    pl.semaphore_wait(barrier, poles + cols - 2)

    def slice_of(index):
        return pl.ds(pl.multiple_of(index * part, part), part)

    def to_pole(src, dst, hop, send, recv):
        return pltpu.make_async_remote_copy(
            src_ref=src,
            dst_ref=dst,
            send_sem=send,
            recv_sem=recv,
            device_id={"pole": (pole + hop) % poles},
            device_id_type=MESH,
        )

    def to_col(src, dst, hop, send, recv):
        return pltpu.make_async_remote_copy(
            src_ref=src,
            dst_ref=dst,
            send_sem=send,
            recv_sem=recv,
            device_id={"col": (col + hop) % cols},
            device_id_type=MESH,
        )

    hops = sorted(range(1, poles), key=lambda h: -min(h, poles - h))
    first, first_diag = {}, {}
    for hop in hops:
        there = slice_of((pole + hop) % poles)
        first[hop] = to_pole(blocks_ref.at[:, there, :], block_in.at[hop], hop, send_a.at[hop], recv_a.at[hop])
        first[hop].start()
    for hop in hops:
        there = slice_of((pole + hop) % poles)
        first_diag[hop] = to_pole(diag_ref.at[:, there, :], diag_in.at[hop], hop, send_d.at[hop], recv_d.at[hop])
        first_diag[hop].start()

    here = slice_of(pole)
    total = blocks_ref[:, here, :].astype(jnp.float32)
    for hop in hops:
        first[hop].wait_recv()
        total += block_in[hop].astype(jnp.float32)
    block_sum[...] = total.astype(block_sum.dtype)
    second = {}
    for hop in range(1, cols):
        dest = (col + hop) % cols
        second[hop] = to_col(
            block_sum.at[pl.ds(dest * CAP, CAP)],
            block_full.at[pl.ds(col * CAP, CAP), here, :],
            hop,
            send_b.at[hop],
            recv_b.at[hop],
        )
        second[hop].start()
    mine = pl.ds(col * CAP, CAP)
    block_full[mine, here, :] = block_sum[mine]

    third = []

    def spread(back):
        source = (col + cols - back) % cols
        view = block_full.at[pl.ds(source * CAP, CAP), here, :]
        for hop in hops:
            copy = to_pole(view, view, hop, send_c.at[hop, back], recv_c.at[hop, back])
            copy.start()
            third.append(copy)

    spread(0)
    diag_total = diag_ref[:, here, :]
    for hop in hops:
        first_diag[hop].wait_recv()
        diag_total += diag_in[hop]
    diag_col[col] = diag_total
    second_diag = {}
    for hop in range(1, cols):
        second_diag[hop] = to_col(
            diag_col.at[col], diag_col.at[col], hop, send_e.at[hop], recv_e.at[hop]
        )
    for hop in range(1, cols):
        second[hop].wait_recv()
        spread(hop)
    for hop in range(1, cols):
        second_diag[hop].start()
    for hop in range(1, cols):
        second_diag[hop].wait_recv()
    diag_total = diag_col[0]
    for c in range(1, cols):
        diag_total += diag_col[c]
    diag_full[:, here, :] = diag_total
    third_diag = []
    for hop in hops:
        view = diag_full.at[:, here, :]
        copy = to_pole(view, view, hop, send_f.at[hop], recv_f.at[hop])
        copy.start()
        third_diag.append(copy)
    for copy in third:
        copy.wait_recv()

    tile_count, list_size = rows_ref.shape[0], rows_ref.shape[1]
    panel_count = panels_ref.shape[1]
    id_count = ids_ref.shape[0]

    def one(t, carry):
        total = jnp.zeros((1, rows_ref.shape[3]), jnp.float32)
        count = counts_ref[t]
        for k in range(list_size):
            block = supports_ref[t, k]
            place = jnp.int32(0)
            for c in range(id_count):
                place = jnp.where(ids_ref[c] == block, c, place)
            mixed = jnp.dot(
                block_full[place], panels_ref[t, block % panel_count], preferred_element_type=jnp.float32
            )
            term = jnp.sum(rows_ref[t, k].astype(jnp.float32) * mixed, axis=0, keepdims=True)
            total += jnp.where(k < count, term, 0.0)
        valence_ref[pl.ds(t, 1), :] = total
        return carry

    lax.fori_loop(0, tile_count, one, 0)
    clamped = jnp.maximum(core_ref[...] + valence_ref[...], density_floor)
    potential_ref[...] = -exchange_coeff * jnp.exp(jnp.log(clamped) * (1.0 / 3.0))

    for copy in third_diag:
        copy.wait_recv()
    diag_out_ref[...] = diag_full[...]
    for group in (first, first_diag, second, second_diag):
        for copy in group.values():
            copy.wait_send()
    for copy in third + third_diag:
        copy.wait_send()


def body(
    inverse,
    panels,
    diag_inverse,
    pole_weights,
    supports,
    counts,
    panel_order,
    row_orbitals,
    panel_orbitals,
    core_density,
):
    rows = inverse.shape[2]
    panel_count, width = panels.shape[1], panels.shape[4]
    cols = lax.axis_size("col")
    me = lax.axis_index("col")
    block_rows = rows // width
    per_device = block_rows * panel_count
    tile_count, list_size = row_orbitals.shape[0], row_orbitals.shape[1]
    total = cols * per_device

    all_ids = jnp.arange(total, dtype=jnp.int32)
    live = jnp.arange(list_size, dtype=jnp.int32)[None, :] < counts[:, None]
    listed = jnp.where(live, supports, -1).reshape(cols, tile_count * list_size)
    needed = jnp.any(listed[:, :, None] == all_ids[None, None, :], axis=1)
    before = (all_ids[:, None] < all_ids[None, :]) & (
        all_ids[:, None] // per_device == all_ids[None, :] // per_device
    )
    rank = jnp.sum(jnp.where(needed[:, :, None] & before[None], 1, 0), axis=1)
    slot = jnp.where(needed, all_ids[None, :] // per_device * CAP + rank, -1)
    ids = jnp.max(
        jnp.where(
            slot[:, None, :] == jnp.arange(cols * CAP, dtype=jnp.int32)[None, :, None], all_ids[None, None, :], -1
        ),
        axis=2,
    )
    mine = lax.dynamic_slice_in_dim(ids, me * CAP, CAP, 1).reshape(-1)
    local = jnp.maximum(mine - me * per_device, 0)
    column = local % panel_count
    source = jnp.zeros_like(column)
    for j in range(panel_count):
        source = jnp.where(column == j, panel_order[j], source)
    chosen = source * block_rows + local // panel_count
    my_ids = lax.dynamic_slice_in_dim(ids, me, 1, 0)[0]
    my_supports = lax.dynamic_slice_in_dim(supports, me * tile_count, tile_count, 0)
    my_counts = lax.dynamic_slice_in_dim(counts, me * tile_count, tile_count, 0)

    pieces = rows // 256 if rows % 256 == 0 else 1
    piece = rows // pieces
    chips = cols // CORES
    slots = 4
    smem = pl.BlockSpec(memory_space=pltpu.SMEM)
    vmem = pl.BlockSpec(memory_space=pltpu.VMEM)
    anywhere = pl.BlockSpec(memory_space=pl.ANY)
    blocks, diag_term = pl.pallas_call(
        functools.partial(panel_kernel, cols, pieces),
        out_shape=(
            jax.ShapeDtypeStruct((cols * CAP, width, width), jnp.bfloat16),
            jax.ShapeDtypeStruct((panel_count, width, width), jnp.float32),
        ),
        in_specs=[smem, smem, smem, anywhere, anywhere, vmem],
        out_specs=(vmem, vmem),
        scratch_shapes=[
            pltpu.VMEM((cols, panel_count, 2, rows, width), jnp.bfloat16),
            pltpu.VMEM((slots, 2, rows, piece), jnp.bfloat16),
            pltpu.VMEM((panel_count, 2 * rows, 2 * width), jnp.float32),
            pltpu.VMEM((per_device, width, width), jnp.float32),
            pltpu.VMEM((panel_count, width, width), jnp.float32),
            pltpu.SemaphoreType.DMA,
            pltpu.SemaphoreType.DMA((slots,)),
            pltpu.SemaphoreType.DMA((chips, pieces)),
            pltpu.SemaphoreType.DMA((chips, pieces)),
            pltpu.SemaphoreType.DMA((chips, pieces)),
            pltpu.SemaphoreType.DMA((chips, pieces)),
        ],
        compiler_params=pltpu.CompilerParams(
            collective_id=0, has_side_effects=True, vmem_limit_bytes=48 * 1024 * 1024
        ),
        name="panel_products",
    )(panel_order, chosen, pole_weights, inverse[0], panels[0], diag_inverse[0])

    poles = lax.axis_size("pole")
    part = width // poles
    chosen_count = cols * CAP
    dma = pltpu.SemaphoreType.DMA
    valence, potential, diag_density = pl.pallas_call(
        functools.partial(exchange_kernel, poles, cols),
        out_shape=(
            jax.ShapeDtypeStruct(core_density.shape, jnp.float32),
            jax.ShapeDtypeStruct(core_density.shape, jnp.float32),
            jax.ShapeDtypeStruct(diag_term.shape, jnp.float32),
        ),
        in_specs=[smem, smem, smem, vmem, vmem, vmem, vmem, vmem],
        out_specs=(vmem, vmem, vmem),
        scratch_shapes=[
            pltpu.VMEM((poles, chosen_count, part, width), jnp.bfloat16),
            pltpu.VMEM((chosen_count, part, width), jnp.bfloat16),
            pltpu.VMEM((chosen_count, width, width), jnp.bfloat16),
            pltpu.VMEM((poles, panel_count, part, width), jnp.float32),
            pltpu.VMEM((cols, panel_count, part, width), jnp.float32),
            pltpu.VMEM((panel_count, width, width), jnp.float32),
            dma((poles,)),
            dma((poles,)),
            dma((cols,)),
            dma((cols,)),
            dma((poles, cols)),
            dma((poles, cols)),
            dma((poles,)),
            dma((poles,)),
            dma((cols,)),
            dma((cols,)),
            dma((poles,)),
            dma((poles,)),
        ],
        compiler_params=pltpu.CompilerParams(
            collective_id=1, has_side_effects=True, vmem_limit_bytes=24 * 1024 * 1024
        ),
        name="block_exchange",
    )(my_ids, my_supports, my_counts, blocks, diag_term, row_orbitals, panel_orbitals, core_density)
    return (valence, potential, diag_density)


def solution(mesh):
    placed = (
        P(("job", "pole"), None, "col", None),
        P(("job", "pole"), None, None, "col", None),
        P(("job", "pole"), None, None, None, None),
        P(("job", "pole"), None),
        P(),
        P(),
        P(),
        P(("job", "col"), None, None, "pole"),
        P(("job", "col"), None, None, "pole"),
        P(("job", "col"), "pole"),
    )
    return jax.shard_map(
        body,
        mesh=mesh,
        in_specs=placed,
        out_specs=(P(("job", "col"), "pole"), P(("job", "col"), "pole"), P("job", None, None)),
        check_vma=False,
    )
```
